512 devices in a mesh: rep: 8 (over y, core), dp: 64 (over x, z).
Axes of the slice: x: 4, y: 4, z: 16, core: 2. Of those that a mesh axis runs over, the one named last changes fastest.
Arguments:
- grads: bfloat16 [8, 64, 1048576], P('rep', None, 'dp'), may hold values from -5 to 5
- owner: int32 [64], replicated, may hold values from 0 to 63, as said below
- left_root: bfloat16 [64, 3, 1024, 1024], P('dp', None, 'rep'), may hold values from -0.1875 to 0.1875
- right_root: bfloat16 [64, 3, 1024, 1024], P('dp', None, None, 'rep'), may hold values from -0.1875 to 0.1875
- momentum: float32 [64, 1048576], P(None, ('rep', 'dp')), may hold values from -6 to 6
- step: int32 [], replicated, may hold values from 1 to 3
Outputs:
- fresh: float32 [64, 1048576], P(None, ('rep', 'dp'))
- update: bfloat16 [64, 1048576], P(None, ('rep', 'dp'))
The draws below stay inside these ranges and needn't reach their ends.
Inputs may be any that keep to these rules, and one draw needn't show every extreme that they name: `owner`: A quarter of the owners hold 3 blocks each, a quarter hold 1, the rest none; which owners and which blocks are drawn from the seed.
All inputs are finite; a program needn't handle non-finite values.
Results may differ from the reference program's by a relative error of at most 0.017.
Values may be sent and summed in bfloat16 or wider, within the bound.
A program may use at most 64 MiB of HBM per device.

```python
import jax
import jax.numpy as jnp
from jax import lax

BLOCK = 1024
BPO = 1
MOST = 3
NB = 64
REPLICAS = 8
N_DP = 64


def draw_owner(key, part):
    key = jax.random.fold_in(key, 7)
    owner_key = jax.random.fold_in(key, 1)
    block_key = jax.random.fold_in(key, 2)
    position = jnp.arange(NB, dtype=jnp.int32)
    group = position // (4 * BPO)
    within = position % (4 * BPO)
    owner_pos = 4 * group + jnp.where(within < 3 * BPO, 0, 1)
    owner_perm = jax.random.permutation(owner_key, N_DP).astype(jnp.int32)
    owners = owner_perm[owner_pos]
    block_perm = jax.random.permutation(block_key, NB).astype(jnp.int32)
    return owners[block_perm].astype(jnp.int32)


def levels(rng, dims, pieces, smallest, top_value):
    def one(dim, parts):
        steps = jax.random.uniform(jax.random.fold_in(jax.random.fold_in(rng, 6), dim), (parts,), jnp.float32, smallest / len(pieces), top_value / len(pieces))
        return jnp.repeat(jnp.exp(steps), dims[dim] // parts).reshape((-1,) + (1,) * (len(dims) - dim - 1))

    factor_of = one(*pieces[0])
    for cut in pieces[1:]:
        factor_of = factor_of * one(*cut)
    return factor_of


def scatter_about(rng, dims, spread, bound, split=(), kind=jnp.bfloat16):
    entries = spread * jax.random.normal(rng, dims, jnp.float32)
    if split:
        entries = entries * levels(rng, dims, split, -0.22, 0.18)
    return jnp.clip(entries, -bound, bound).astype(kind)


def setup_inputs(seed: int = 0) -> dict:
    splits = jax.random.split(jax.random.key(seed), 7)
    grads = scatter_about(splits[0], (REPLICAS, NB, BLOCK * BLOCK), 0.35, 5.0, ((0, 8), (2, 64)))
    owner = draw_owner(jax.random.fold_in(splits[6], 71), 0)
    left_root = scatter_about(splits[2], (N_DP, MOST, BLOCK, BLOCK), BLOCK ** -0.5, 0.1875, ((0, 64), (2, 8)))
    right_root = scatter_about(splits[3], (N_DP, MOST, BLOCK, BLOCK), BLOCK ** -0.5, 0.1875, ((0, 64), (3, 8)))
    momentum = scatter_about(splits[4], (NB, BLOCK * BLOCK), 1.0, 6.0, ((1, 512),), jnp.float32)
    step = jax.random.randint(splits[5], (), 1, 4).astype(jnp.int32)
    return dict(grads=grads, owner=owner, left_root=left_root, right_root=right_root, momentum=momentum, step=step)


decay_rate = 0.5


def slots_of(owner):
    order = jnp.arange(owner.shape[0], dtype=jnp.int32)
    same = (owner[:, None] == owner[None, :]) & (order[None, :] < order[:, None])
    return jnp.sum(same.astype(jnp.int32), axis=1).astype(jnp.int32)


def reference(grads, owner, left_root, right_root, momentum, step):
    slot = slots_of(owner)

    def one_block(block_id):
        summed = jnp.sum(grads[:, block_id].astype(jnp.float32), axis=0).astype(jnp.bfloat16)
        summed = summed.reshape(BLOCK, BLOCK)
        holder = owner[block_id]
        place = slot[block_id]
        right_mat = right_root[holder, place]
        left_mat = left_root[holder, place]
        partial_value = jnp.dot(summed, right_mat, preferred_element_type=jnp.float32).astype(jnp.bfloat16)
        result = jnp.dot(left_mat, partial_value, preferred_element_type=jnp.float32).astype(jnp.bfloat16)
        return result.reshape(BLOCK * BLOCK)

    direction = lax.map(one_block, jnp.arange(NB, dtype=jnp.int32))
    fresh = decay_rate * momentum + (1.0 - decay_rate) * direction.astype(jnp.float32)
    factor = 1.0 - jnp.power(jnp.float32(decay_rate), step.astype(jnp.float32))
    update = (fresh / factor).astype(jnp.bfloat16)
    return fresh, update
```

```python
import functools

import jax
import jax.numpy as jnp
from jax import lax
from jax.experimental import pallas as pl
from jax.experimental.pallas import tpu as pltpu
from jax.sharding import PartitionSpec as P

BLOCK = 1024
MOST = 3
NX, NY, NZ, NR = 4, 4, 16, 8
NB = 64
FULL = NX * MOST
MESH = pl.DeviceIdType.MESH
Z_ORDER = (8, 7, 9, 6, 10, 5, 11, 4, 12, 3, 13, 2, 14, 1, 15)

decay_rate = 0.5


def tables_kernel(owner, blk, pos, ent, fin, most, per_line, per_plane):
    @pl.loop(0, NZ * FULL)
    def _(i):
        blk[i] = 0
        pos[i] = 0
        ent[i] = 0

    @pl.loop(0, NB)
    def _(i):
        per_line[i] = 0

    @pl.loop(0, NZ)
    def _(i):
        per_plane[i] = 0

    def place(b, top):
        line = owner[b]
        x, z = line // NZ, line % NZ
        s = per_line[line]
        e = per_plane[z]
        per_line[line] = s + 1
        per_plane[z] = e + 1
        blk[z * FULL + e] = b
        pos[z * FULL + x * MOST + s] = e
        ent[z * FULL + e] = s * NX + x
        fin[b] = z * 16 + e
        return jnp.maximum(top, e + 1)

    most[0] = lax.fori_loop(0, NB, place, jnp.int32(0))


def tables(owner):
    smem = pl.BlockSpec(memory_space=pltpu.SMEM)
    table = jax.ShapeDtypeStruct((NZ * FULL,), jnp.int32)
    return pl.pallas_call(
        tables_kernel,
        out_shape=(
            table,
            table,
            table,
            jax.ShapeDtypeStruct((NB,), jnp.int32),
            jax.ShapeDtypeStruct((1,), jnp.int32),
        ),
        in_specs=[smem],
        out_specs=(smem,) * 5,
        scratch_shapes=[pltpu.SMEM((NB,), jnp.int32), pltpu.SMEM((NZ,), jnp.int32)],
        name="tables",
    )(owner)


def step_kernel(
    cap, grads, left, right, blk, pos, ent, fin, out,
    gbuf, s_a, r_a, s_b, r_b, tsc, gt, s_z, r_z, s_x, gcol, lfull, rfull,
    s_w, r_w, s_e, r_e, s_q, r_q,
    load_sem, a1s, a1r, a2s, a2r, z1s, z1r, x1s, x1r, ns, nr, hs, hr, cs, cr, ws, wr, e1s, e1r, e2s, e2r,
):
    rep, dp = lax.axis_index("rep"), lax.axis_index("dp")
    y, c = rep // 2, rep % 2
    x, z = dp // NZ, dp % NZ

    def at(dx=0, dy=0, dz=0, dc=0):
        return (((y + dy) % NY) * 2 + (c + dc) % 2, ((x + dx) % NX) * NZ + (z + dz) % NZ)

    def remote(src, dst, send, recv, device):
        return pltpu.make_async_remote_copy(
            src_ref=src, dst_ref=dst, send_sem=send, recv_sem=recv, device_id=device, device_id_type=MESH
        )

    load_g = pltpu.make_async_copy(grads.at[0], gbuf, load_sem.at[0])
    load_g.start()
    load_l = pltpu.make_async_copy(left.at[0], lfull.at[:, rep], load_sem.at[1])
    load_l.start()
    load_r = pltpu.make_async_copy(right.at[0], rfull.at[:, rep], load_sem.at[2])
    load_r.start()

    with jax.named_scope("barrier"):
        barrier = pltpu.get_barrier_semaphore()
        peers = [at(dy=k // 2, dc=k % 2) for k in range(1, NR)]
        peers += [at(dx=k) for k in range(1, NX)]
        peers += [at(dz=k) for k in range(1, NZ)]
        for peer in peers:
            pl.semaphore_signal(barrier, inc=1, device_id=peer, device_id_type=MESH)
        pl.semaphore_wait(barrier, len(peers))

    def chunk(j, k, core):
        column = 8 * j + 2 * ((y + k) % NY) + core
        return gbuf[:, pl.ds(pl.multiple_of(128 * column, 128), 128)]

    a1 = [remote(s_a.at[k], r_a.at[k], a1s.at[k], a1r.at[k], at(dc=1)) for k in range(NY)]
    a2 = {k: remote(s_b.at[k], r_b.at[k], a2s.at[k], a2r.at[k], at(dy=k)) for k in (1, 2, 3)}
    with jax.named_scope("pair_sum"):
        load_g.wait()
        for k in (2, 1, 3, 0):

            @pl.loop(0, 16)
            def _(j, k=k):
                s_a[k, j] = chunk(j, k, 1 - c)

            a1[k].start()
        for k in (2, 1, 3):
            a1[k].wait_recv()

            @pl.loop(0, 16)
            def _(j, k=k):
                total = chunk(j, k, c).astype(jnp.float32) + r_a[k, j].astype(jnp.float32)
                s_b[k, j] = total.astype(jnp.bfloat16)

            a2[k].start()
    with jax.named_scope("y_sum"):
        a1[0].wait_recv()
        for k in (1, 2, 3):
            a2[k].wait_recv()

        @pl.loop(0, 16)
        def _(j):
            total = chunk(j, 0, c).astype(jnp.float32) + r_a[0, j].astype(jnp.float32)
            for k in (1, 2, 3):
                total += r_b[k, j].astype(jnp.float32)
            tsc[pl.ds(j, NB, stride=16), :] = total

        gt[...] = tsc[...].astype(jnp.bfloat16).reshape(NB, 16, 128)

    z1 = {k: remote(s_z.at[k], r_z.at[k], z1s.at[k], z1r.at[k], at(dz=k)) for k in range(1, NZ)}
    with jax.named_scope("to_plane"):
        for k in Z_ORDER + (0,):

            @pl.loop(0, cap)
            def _(e, k=k):
                tile = gt[blk[((z + k) % NZ) * FULL + e]]
                if k:
                    s_z[k, e] = tile
                else:
                    r_z[0, e] = tile

            if k:
                z1[k].start()

    def part(m, r, half=None):
        ref = (lfull if m < MOST else rfull).at[m % MOST, r]
        rows = 128 if m < MOST else 1024
        return ref if half is None else ref.at[pl.ds(half * (rows // 2), rows // 2)]

    def rep_of(dy, core):
        return ((y + dy) % NY) * 2 + core

    def near(m, up):
        return remote(part(m, rep), part(m, rep), ns.at[m, up], nr.at[m, up], at(dy=1 if up else 3))

    def near_in(m, up):
        r = rep_of(3 if up else 1, c)
        return remote(part(m, r), part(m, r), ns.at[m, up], nr.at[m, up], at(dy=1 if up else 3))

    def far(m, up):
        r = rep_of(3 if up else 1, c)
        return remote(part(m, r, up), part(m, r, up), hs.at[m, up], hr.at[m, up], at(dy=1 if up else 3))

    def far_in(m, up):
        r = rep_of(2, c)
        return remote(part(m, r, up), part(m, r, up), hs.at[m, up], hr.at[m, up], at(dy=1 if up else 3))

    def cross(m, k):
        r = rep_of(k, c)
        return remote(part(m, r), part(m, r), cs.at[m, k], cr.at[m, k], at(dc=1))

    def cross_in(m, k):
        r = rep_of(k, 1 - c)
        return remote(part(m, r), part(m, r), cs.at[m, k], cr.at[m, k], at(dc=1))

    def gather_start(ms):
        for m in ms:
            near(m, 1).start()
            near(m, 0).start()
            cross(m, 0).start()

    def gather_forward(ms):
        for m in ms:
            near_in(m, 1).wait_recv()
            far(m, 1).start()
            cross(m, 3).start()
            near_in(m, 0).wait_recv()
            far(m, 0).start()
            cross(m, 1).start()

    def gather_last(ms):
        for m in ms:
            far_in(m, 1).wait_recv()
            far_in(m, 0).wait_recv()
            cross(m, 2).start()

    def gather_done(ms):
        for m in ms:
            for k in range(NY):
                cross_in(m, k).wait_recv()

    lefts, rights = range(MOST), range(MOST, 2 * MOST)
    with jax.named_scope("left_start"):
        load_l.wait()
        gather_start(lefts)
    with jax.named_scope("left_forward"):
        gather_forward(lefts)
    load_r.wait()
    gather_start(rights)

    def x1(k, s):
        return remote(s_x.at[k, s], gcol.at[s, x], x1s.at[s, k], x1r.at[s, k], at(dx=k))

    def x1_in(k, s):
        return remote(s_x.at[k, s], gcol.at[s, (x + NX - k) % NX], x1s.at[s, k], x1r.at[s, k], at(dx=k))

    with jax.named_scope("at_plane"):
        for k in range(1, NZ):
            z1[k].wait_recv()
    with jax.named_scope("to_owner"):
        for s in range(MOST):
            for k in (2, 1, 3, 0):
                to = (x + k) % NX

                @pl.loop(0, NZ)
                def _(i, s=s, k=k, to=to):
                    tile = r_z[i, pos[z * FULL + to * MOST + s]]
                    rows = pl.ds(pl.multiple_of(16 * ((z + NZ - i) % NZ), 16), 16)
                    if k:
                        s_x[k, s, rows] = tile
                    else:
                        gcol[s, x, rows] = tile

                if k:
                    x1(k, s).start()
    with jax.named_scope("left_last"):
        gather_last(lefts)
        gather_done(lefts)

    def w1(k, s):
        r = rep_of(k // 2, (c + k) % 2)
        return remote(s_w.at[s, r], r_w.at[s, rep], ws.at[s, k], wr.at[s, k], at(dy=k // 2, dc=k % 2))

    def w1_in(k, s):
        r = rep_of(NY - k // 2, (c + k) % 2)
        return remote(s_w.at[s, r], r_w.at[s, r], ws.at[s, k], wr.at[s, k], at(dy=k // 2, dc=k % 2))

    with jax.named_scope("left_product"):
        for s in range(MOST):
            for k in range(1, NX):
                x1_in(k, s).wait_recv()
            g = gcol[s].reshape(BLOCK, 128)

            @pl.loop(0, 2)
            def _(h, s=s, g=g):
                rows = lfull[s, pl.ds(4 * h, 4)].reshape(512, BLOCK)
                w = jnp.dot(rows, g, preferred_element_type=jnp.float32)
                s_w[s, pl.ds(4 * h, 4)] = w.astype(jnp.bfloat16).reshape(4, 128, 128)

            for k in (4, 5, 2, 3, 6, 7, 1):
                w1(k, s).start()
            r_w[s, rep] = s_w[s, rep]
    with jax.named_scope("right_forward"):
        gather_forward(rights)
    with jax.named_scope("right_last"):
        gather_last(rights)
        gather_done(rights)

    def e1(k, s):
        return remote(s_e.at[s, (x + k) % NX], r_e.at[s * NX + x], e1s.at[s, k], e1r.at[s, k], at(dx=k))

    def e1_in(k, s):
        return remote(s_e.at[s, x], r_e.at[s * NX + (x + NX - k) % NX], e1s.at[s, k], e1r.at[s, k], at(dx=k))

    with jax.named_scope("right_product"):
        for s in range(MOST):
            for k in range(1, NR):
                w1_in(k, s).wait_recv()
            w = jnp.concatenate([r_w[s, r] for r in range(NR)], axis=1)
            for p in range(4):
                cols = jnp.concatenate([rfull[s, 2 * p], rfull[s, 2 * p + 1]], axis=1)
                d = jnp.dot(w, cols, preferred_element_type=jnp.float32)
                tsc[pl.ds(2 * p, 128, stride=8), :] = d[:, :128]
                tsc[pl.ds(2 * p + 1, 128, stride=8), :] = d[:, 128:]
            s_e[s] = tsc[...].astype(jnp.bfloat16).reshape(NX, 256, 128)
            for k in (2, 1, 3):
                e1(k, s).start()
            r_e[s * NX + x] = s_e[s, x]

    e2 = {k: remote(s_q.at[k], r_q.at[pl.ds(k * cap, cap)], e2s.at[k], e2r.at[k], at(dz=k)) for k in range(1, NZ)}
    with jax.named_scope("from_owner"):
        for s in range(MOST):
            for k in range(1, NX):
                e1_in(k, s).wait_recv()
    with jax.named_scope("from_plane"):
        for k in Z_ORDER + (0,):
            rows = pl.ds(pl.multiple_of(16 * ((z + k) % NZ), 16), 16)

            @pl.loop(0, cap)
            def _(e, k=k, rows=rows):
                tile = r_e[ent[z * FULL + e], rows]
                if k:
                    s_q[k, e] = tile
                else:
                    r_q[e] = tile

            if k:
                e2[k].start()
        for k in range(1, NZ):
            e2[k].wait_recv()
    with jax.named_scope("pick"):

        @pl.loop(0, NB)
        def _(b):
            v = fin[b]
            tile = r_q[((z + NZ - v // 16) % NZ) * cap + v % 16]
            tsc[pl.ds(pl.multiple_of(16 * b, 16), 16), :] = tile.astype(jnp.float32)

        for j in range(16):
            out[:, 128 * j : 128 * (j + 1)] = tsc[pl.ds(j, NB, stride=16), :].astype(jnp.bfloat16)

    with jax.named_scope("sends_done"):
        for k in range(NY):
            a1[k].wait_send()
        for k in (1, 2, 3):
            a2[k].wait_send()
        for k in range(1, NZ):
            z1[k].wait_send()
            e2[k].wait_send()
        for s in range(MOST):
            for k in range(1, NX):
                x1(k, s).wait_send()
                e1(k, s).wait_send()
            for k in range(1, NR):
                w1(k, s).wait_send()
        for m in range(2 * MOST):
            for up in range(2):
                near(m, up).wait_send()
                far(m, up).wait_send()
            for k in range(NY):
                cross(m, k).wait_send()


def directions(cap, cid, grads, left, right, blk, pos, ent, fin):
    bf16, f32, dma = jnp.bfloat16, jnp.float32, pltpu.SemaphoreType.DMA
    hbm = pl.BlockSpec(memory_space=pl.ANY)
    smem = pl.BlockSpec(memory_space=pltpu.SMEM)
    return pl.pallas_call(
        functools.partial(step_kernel, cap),
        out_shape=jax.ShapeDtypeStruct((NB, 2048), bf16),
        in_specs=[hbm] * 3 + [smem] * 4,
        out_specs=pl.BlockSpec(memory_space=pltpu.VMEM),
        scratch_shapes=[
            pltpu.VMEM((NB, 16384), bf16),
            pltpu.VMEM((NY, 16, NB, 128), bf16),
            pltpu.VMEM((NY, 16, NB, 128), bf16),
            pltpu.VMEM((NY, 16, NB, 128), bf16),
            pltpu.VMEM((NY, 16, NB, 128), bf16),
            pltpu.VMEM((BLOCK, 128), f32),
            pltpu.VMEM((NB, 16, 128), bf16),
            pltpu.VMEM((NZ, cap, 16, 128), bf16),
            pltpu.VMEM((NZ, cap, 16, 128), bf16),
            pltpu.VMEM((NX, MOST, 256, 128), bf16),
            pltpu.VMEM((MOST, NX, 256, 128), bf16),
            pltpu.VMEM((MOST, NR, 128, BLOCK), bf16),
            pltpu.VMEM((MOST, NR, BLOCK, 128), bf16),
            pltpu.VMEM((MOST, NR, 128, 128), bf16),
            pltpu.VMEM((MOST, NR, 128, 128), bf16),
            pltpu.VMEM((MOST, NX, 256, 128), bf16),
            pltpu.VMEM((MOST * NX, 256, 128), bf16),
            pltpu.VMEM((NZ, cap, 16, 128), bf16),
            pltpu.VMEM((NZ * cap, 16, 128), bf16),
            dma((3,)),
            dma((NY,)), dma((NY,)),
            dma((NY,)), dma((NY,)),
            dma((NZ,)), dma((NZ,)),
            dma((MOST, NX)), dma((MOST, NX)),
            dma((2 * MOST, 2)), dma((2 * MOST, 2)),
            dma((2 * MOST, 2)), dma((2 * MOST, 2)),
            dma((2 * MOST, NY)), dma((2 * MOST, NY)),
            dma((MOST, NR)), dma((MOST, NR)),
            dma((MOST, NX)), dma((MOST, NX)),
            dma((NZ,)), dma((NZ,)),
        ],
        compiler_params=pltpu.CompilerParams(
            collective_id=cid, has_side_effects=True, vmem_limit_bytes=48 * 2**20
        ),
        name=f"directions_{cap}",
    )(grads, left, right, blk, pos, ent, fin)


CAPS = (12,)


def body(grads, owner, left_root, right_root, momentum, step):
    blk, pos, ent, fin, most = tables(owner)
    args = (grads, left_root, right_root, blk, pos, ent, fin)
    if len(CAPS) == 1:
        mine = directions(CAPS[0], 0, *args)
    else:
        which = sum((most[0] > cap).astype(jnp.int32) for cap in CAPS[:-1])
        mine = lax.switch(which, [functools.partial(directions, cap, i) for i, cap in enumerate(CAPS)], *args)
    fresh = decay_rate * momentum + (1.0 - decay_rate) * mine.astype(jnp.float32)
    factor = 1.0 - jnp.power(jnp.float32(decay_rate), step.astype(jnp.float32))
    update = (fresh / factor).astype(jnp.bfloat16)
    return (fresh, update)


def solution(mesh):
    return jax.shard_map(
        body,
        mesh=mesh,
        in_specs=(
            P("rep", None, "dp"),
            P(),
            P("dp", None, "rep", None),
            P("dp", None, None, "rep"),
            P(None, ("rep", "dp")),
            P(),
        ),
        out_specs=(P(None, ("rep", "dp")), P(None, ("rep", "dp"))),
        check_vma=False,
    )
```

```python
import functools

import jax
import jax.numpy as jnp
from jax import lax
from jax.experimental import pallas as pl
from jax.experimental.pallas import tpu as pltpu
from jax.sharding import PartitionSpec as P

BLOCK = 1024
MOST = 3
NX, NY, NZ, NR = 4, 4, 16, 8
NB = 64
MESH = pl.DeviceIdType.MESH
Z_ORDER = (8, 7, 9, 6, 10, 5, 11, 4, 12, 3, 13, 2, 14, 1, 15)
GATE = Z_ORDER[:7]


decay_rate = 0.5


def block_tables(cap, owner, tab):
    def spread(b, both):
        row, col = both
        return jnp.where(lane == b, owner[b], row), jnp.where(sub == b, owner[b], col)

    sub = lax.broadcasted_iota(jnp.int32, (NB, 128), 0)
    lane = lax.broadcasted_iota(jnp.int32, (NB, 128), 1)
    none = jnp.full((NB, 128), -1, jnp.int32)
    row, col = lax.fori_loop(0, NB, spread, (none, none))
    one = jnp.ones((NB, 128), jnp.int32)
    held = row >= 0
    same = held & (row == col)
    slot = jnp.sum(jnp.where(same & (lane < sub), one, 0), axis=1, keepdims=True)
    slot_row = jnp.sum(jnp.where(same & (sub < lane), one, 0), axis=0, keepdims=True)
    peers = held & ((row & 15) == (col & 15)) & (slot_row == slot) & (row < col)
    rank = jnp.sum(jnp.where(peers, one, 0), axis=1, keepdims=True)
    line = col[:, :1]
    x, z = line // NZ, line & 15
    j = jnp.where(slot == 0, x, jnp.minimum(rank, cap - 1))
    place = z * 16 + jnp.minimum(slot, MOST - 1) * 4 + j
    block = lax.broadcasted_iota(jnp.int32, (NB, 1), 0)
    index = lax.broadcasted_iota(jnp.int32, (NB, 256), 1)
    tab[...] = jnp.zeros_like(tab)
    rows = (
        (place, block, NB - 1),
        (z * 16 + slot * 4 + x, j, cap - 1),
        (place, x, NX - 1),
        (block, place, NZ * 16 - 1),
    )
    for i, (key, value, top) in enumerate(rows):
        tab[i : i + 1, :] = jnp.minimum(jnp.sum(jnp.where(index == key, value, 0), axis=0, keepdims=True), top)


def step_kernel(
    cap, grads, left, right, owner_in, out,
    owner, vtab, tab, gbuf, s_a, r_a, s_b, r_b, tsc, gt, s_z, r_z0, r_z1, r_z2, s_x, gfull, lrow, rfull,
    s_e, r_e0, r_e1, r_e2, s_q, r_q,
    load_sem, a1s, a1r, a2s, a2r, z1s, z1r, x1s, x1r, ns, nr, hs, hr, cs, cr, e1s, e1r, e2s, e2r,
):
    caps = (NX, cap, cap)
    starts = (0, NX, NX + cap)
    rep, dp = lax.axis_index("rep"), lax.axis_index("dp")
    y, c = rep // 2, rep % 2
    x, z = dp // NZ, dp % NZ

    def at(dx=0, dy=0, dz=0, dc=0):
        return (((y + dy) % NY) * 2 + (c + dc) % 2, ((x + dx) % NX) * NZ + (z + dz) % NZ)

    def remote(src, dst, send, recv, device):
        return pltpu.make_async_remote_copy(
            src_ref=src, dst_ref=dst, send_sem=send, recv_sem=recv, device_id=device, device_id_type=MESH
        )

    load_o = pltpu.make_async_copy(owner_in, owner, load_sem.at[3])
    load_o.start()
    load_g = pltpu.make_async_copy(grads.at[0], gbuf, load_sem.at[0])
    load_g.start()
    load_l = pltpu.make_async_copy(left.at[0], lrow, load_sem.at[1])
    load_l.start()
    load_r = pltpu.make_async_copy(right.at[0], rfull.at[:, rep], load_sem.at[2])
    load_r.start()

    barrier = pltpu.get_barrier_semaphore()
    peers = [at(dz=k) for k in Z_ORDER] + [at(dx=k) for k in (2, 1, 3)]
    peers += [at(dy=k) for k in (1, 2, 3)] + [at(dc=1)]
    for peer in peers:
        pl.semaphore_signal(barrier, inc=1, device_id=peer, device_id_type=MESH)

    links = {}
    loads = {"left": load_l, "right": load_r, "owner": load_o}

    def go(name, out, back):
        out.start()
        links[name] = [out, back, True, True]

    def arrive(*name):
        links[name][1].wait_recv()
        links[name][2] = False

    def left(*name):
        links[name][0].wait_send()
        links[name][3] = False

    def loaded(name):
        loads.pop(name).wait()

    def finish():
        for copy in loads.values():
            copy.wait()
        for out, back, due, sent in links.values():
            if due:
                back.wait_recv()
            if sent:
                out.wait_send()

    def chunk(j, k, core):
        column = 8 * j + 2 * ((y + k) % NY) + core
        return gbuf[:, pl.ds(pl.multiple_of(128 * column, 128), 128)]

    def part(m, r, half=None):
        if m < MOST:
            return rfull.at[m, r] if half is None else rfull.at[m, r, pl.ds(half * 512, 512)]
        return gfull.at[m - MOST, r] if half is None else gfull.at[m - MOST, r, pl.ds(2 * half, 2)]

    def rep_of(dy, core):
        return ((y + dy) % NY) * 2 + core

    def near(m):
        for up in (1, 0):

            def copy(r, up=up):
                return remote(part(m, r), part(m, r), ns.at[m, up], nr.at[m, up], at(dy=1 if up else 3))

            go(("near", m, up), copy(rep), copy(rep_of(3 if up else 1, c)))
        cross(m, 0)

    def far(m, up):
        def copy(r):
            return remote(part(m, r, up), part(m, r, up), hs.at[m, up], hr.at[m, up], at(dy=1 if up else 3))

        go(("far", m, up), copy(rep_of(3 if up else 1, c)), copy(rep_of(2, c)))

    def cross(m, k):
        def copy(core):
            r = rep_of(k, core)
            return remote(part(m, r), part(m, r), cs.at[m, k], cr.at[m, k], at(dc=1))

        go(("cross", m, k), copy(c), copy(1 - c))

    def forward(m):
        for up in (1, 0):
            arrive("near", m, up)
            far(m, up)
        cross(m, 3)
        cross(m, 1)

    def last(m):
        arrive("far", m, 1)
        arrive("far", m, 0)
        cross(m, 2)

    def whole(m):
        for k in range(NY):
            arrive("cross", m, k)

    with jax.named_scope("pair_pack"):
        load_g.wait()
        for k in (2, 1, 3, 0):

            @pl.loop(0, 16)
            def _(j, k=k):
                s_a[k, j] = chunk(j, k, 1 - c)

    with jax.named_scope("barrier"):
        pl.semaphore_wait(barrier, len(peers))

    with jax.named_scope("pair_sum"):
        for k in (2, 1, 3, 0):
            copy = remote(s_a.at[k], r_a.at[k], a1s.at[k], a1r.at[k], at(dc=1))
            go(("a1", k), copy, copy)
        loaded("right")
        near(0)
        for k in (2, 1, 3):
            arrive("a1", k)

            @pl.loop(0, 16)
            def _(j, k=k):
                total = chunk(j, k, c).astype(jnp.float32) + r_a[k, j].astype(jnp.float32)
                s_b[k, j] = total.astype(jnp.bfloat16)

            copy = remote(s_b.at[k], r_b.at[k], a2s.at[k], a2r.at[k], at(dy=k))
            go(("a2", k), copy, copy)

    with jax.named_scope("tables"):
        loaded("owner")
        block_tables(cap, owner, vtab)
        to_smem = pltpu.make_async_copy(vtab, tab, load_sem.at[4])
        to_smem.start()
        loads["tables"] = to_smem

    with jax.named_scope("y_sum"):
        arrive("a1", 0)
        for k in (1, 2, 3):
            arrive("a2", k)

        @pl.loop(0, 16)
        def _(j):
            total = chunk(j, 0, c).astype(jnp.float32) + r_a[0, j].astype(jnp.float32)
            for k in (1, 2, 3):
                total += r_b[k, j].astype(jnp.float32)
            tsc[pl.ds(j, NB, stride=16), :] = total

        gt[...] = tsc[...].astype(jnp.bfloat16).reshape(NB, 16, 128)
        loaded("tables")

    r_z, r_e = (r_z0, r_z1, r_z2), (r_e0, r_e1, r_e2)

    def to_plane(s):
        for k in Z_ORDER + (0,):

            @pl.loop(0, caps[s])
            def _(e, k=k):
                tile = gt[tab[0, ((z + k) % NZ) * 16 + 4 * s + e]]
                if k:
                    s_z[k, starts[s] + e] = tile
                else:
                    r_z[s][0, e] = tile

            if k:
                copy = remote(s_z.at[k, pl.ds(starts[s], caps[s])], r_z[s].at[k], z1s.at[s, k], z1r.at[s, k], at(dz=k))
                go(("z1", s, k), copy, copy)

    def to_owner(s):
        for k in range(1, NZ):
            arrive("z1", s, k)
        for k in (2, 1, 3, 0):
            to = (x + k) % NX

            @pl.loop(0, NZ)
            def _(i, k=k, to=to):
                tile = r_z[s][i, tab[1, z * 16 + 4 * s + to] if s else to]
                rows = pl.ds(pl.multiple_of(16 * ((z + NZ - i) % NZ), 16), 16)
                if k:
                    s_x[k, s, rows] = tile
                else:
                    gfull[s, rep, x, rows] = tile

            if k:

                def x1(to, k=k):
                    return remote(s_x.at[k, s], gfull.at[s, rep, to], x1s.at[s, k], x1r.at[s, k], at(dx=k))

                go(("x1", s, k), x1(x), x1((x + NX - k) % NX))

    def at_owner(s):
        for k in range(1, NX):
            arrive("x1", s, k)
        near(MOST + s)

    def products(s):
        whole(s)
        whole(MOST + s)
        w = []
        for p in range(4):
            cols = jnp.concatenate([gfull[s, 2 * p + i].reshape(BLOCK, 128) for i in range(2)], axis=1)
            w.append(jnp.dot(lrow[s], cols, preferred_element_type=jnp.float32).astype(jnp.bfloat16))
        w = jnp.concatenate(w, axis=1)
        for p in range(4):
            cols = jnp.concatenate([rfull[s, 2 * p], rfull[s, 2 * p + 1]], axis=1)
            d = jnp.dot(w, cols, preferred_element_type=jnp.float32)
            tsc[pl.ds(2 * p, 128, stride=8), :] = d[:, :128]
            tsc[pl.ds(2 * p + 1, 128, stride=8), :] = d[:, 128:]
        s_e[s] = tsc[...].astype(jnp.bfloat16).reshape(NX, NZ, 16, 128)
        for k in (2, 1, 3):

            def e1(to, come, k=k):
                return remote(s_e.at[s, to], r_e[s].at[come], e1s.at[s, k], e1r.at[s, k], at(dx=k))

            go(("e1", s, k), e1((x + k) % NX, x), e1(x, (x + NX - k) % NX))
        r_e[s][x] = s_e[s, x]

    def from_owner(s):
        for k in range(1, NX):
            arrive("e1", s, k)
        for k in Z_ORDER + (0,):

            @pl.loop(0, caps[s])
            def _(e, k=k):
                tile = r_e[s][tab[2, z * 16 + 4 * s + e] if s else e, (z + k) % NZ]
                if k:
                    s_q[k, starts[s] + e] = tile
                else:
                    r_q[0, starts[s] + e] = tile

            if k:
                mine = pl.ds(starts[s], caps[s])
                copy = remote(s_q.at[k, mine], r_q.at[k, mine], e2s.at[s, k], e2r.at[s, k], at(dz=k))
                go(("e2", s, k), copy, copy)

    def gate(s):
        for k in GATE:
            left("z1", s, k)

    with jax.named_scope("out"):
        to_plane(0)
        near(1)
        near(2)
        forward(0)
    with jax.named_scope("out_1"):
        gate(0)
        to_plane(1)
        forward(1)
        forward(2)
        to_owner(0)
    with jax.named_scope("out_2"):
        gate(1)
        to_plane(2)
        at_owner(0)
        for s in range(MOST):
            last(s)
    with jax.named_scope("gather_0"):
        to_owner(1)
        forward(3)
        at_owner(1)
        last(3)
    with jax.named_scope("product_0"):
        loaded("left")
        products(0)
    with jax.named_scope("gather_1"):
        to_owner(2)
        forward(4)
        at_owner(2)
        from_owner(0)
        last(4)
    with jax.named_scope("product_1"):
        products(1)
        forward(5)
        last(5)
        from_owner(1)
    with jax.named_scope("product_2"):
        products(2)
        from_owner(2)
    with jax.named_scope("at_shards"):
        for s in range(MOST):
            for k in range(1, NZ):
                arrive("e2", s, k)
    with jax.named_scope("pick"):

        @pl.loop(0, NB)
        def _(b):
            v = tab[3, b]
            place = v % 16
            tile = r_q[(z + NZ - v // 16) % NZ, place - (place // 8) * (NX - cap)]
            tsc[pl.ds(pl.multiple_of(16 * b, 16), 16), :] = tile.astype(jnp.float32)

        for j in range(16):
            out[:, 128 * j : 128 * (j + 1)] = tsc[pl.ds(j, NB, stride=16), :].astype(jnp.bfloat16)

    with jax.named_scope("sends_done"):
        finish()


def directions(cap, cid, grads, left, right, owner):
    bf16, f32, dma = jnp.bfloat16, jnp.float32, pltpu.SemaphoreType.DMA
    hbm = pl.BlockSpec(memory_space=pl.ANY)
    return pl.pallas_call(
        functools.partial(step_kernel, cap),
        out_shape=jax.ShapeDtypeStruct((NB, 2048), bf16),
        in_specs=[hbm] * 4,
        out_specs=pl.BlockSpec(memory_space=pltpu.VMEM),
        scratch_shapes=[
            pltpu.SMEM((NB,), jnp.int32),
            pltpu.VMEM((8, 256), jnp.int32),
            pltpu.SMEM((8, 256), jnp.int32),
            pltpu.VMEM((NB, 16384), bf16),
            pltpu.VMEM((NY, 16, NB, 128), bf16),
            pltpu.VMEM((NY, 16, NB, 128), bf16),
            pltpu.VMEM((NY, 16, NB, 128), bf16),
            pltpu.VMEM((NY, 16, NB, 128), bf16),
            pltpu.VMEM((BLOCK, 128), f32),
            pltpu.VMEM((NB, 16, 128), bf16),
            pltpu.VMEM((NZ, NX + 2 * cap, 16, 128), bf16),
            pltpu.VMEM((NZ, NX, 16, 128), bf16),
            pltpu.VMEM((NZ, cap, 16, 128), bf16),
            pltpu.VMEM((NZ, cap, 16, 128), bf16),
            pltpu.VMEM((NX, MOST, 256, 128), bf16),
            pltpu.VMEM((MOST, NR, NX, 256, 128), bf16),
            pltpu.VMEM((MOST, 128, BLOCK), bf16),
            pltpu.VMEM((MOST, NR, BLOCK, 128), bf16),
            pltpu.VMEM((MOST, NX, NZ, 16, 128), bf16),
            pltpu.VMEM((NX, NZ, 16, 128), bf16),
            pltpu.VMEM((NX, NZ, 16, 128), bf16),
            pltpu.VMEM((NX, NZ, 16, 128), bf16),
            pltpu.VMEM((NZ, NX + 2 * cap, 16, 128), bf16),
            pltpu.VMEM((NZ, NX + 2 * cap, 16, 128), bf16),
            dma((5,)),
            dma((NY,)), dma((NY,)),
            dma((NY,)), dma((NY,)),
            dma((MOST, NZ)), dma((MOST, NZ)),
            dma((MOST, NX)), dma((MOST, NX)),
            dma((2 * MOST, 2)), dma((2 * MOST, 2)),
            dma((2 * MOST, 2)), dma((2 * MOST, 2)),
            dma((2 * MOST, NY)), dma((2 * MOST, NY)),
            dma((MOST, NX)), dma((MOST, NX)),
            dma((MOST, NZ)), dma((MOST, NZ)),
        ],
        compiler_params=pltpu.CompilerParams(
            collective_id=cid, has_side_effects=True, vmem_limit_bytes=48 * 2**20
        ),
        name=f"directions_{cap}",
    )(grads, left, right, owner)


CAPS = (3, NX)


def body(grads, owner, left_root, right_root, momentum, step):
    lines = jnp.arange(NX * NZ, dtype=jnp.int32).reshape(NX, NZ, 1)
    held = jnp.sum((owner == lines).astype(jnp.int32), axis=2)
    most = jnp.max(jnp.sum((held > 1).astype(jnp.int32), axis=0))
    which = sum((most > cap).astype(jnp.int32) for cap in CAPS[:-1])
    branches = [functools.partial(directions, cap, i) for i, cap in enumerate(CAPS)]
    mine = lax.switch(which, branches, grads, left_root, right_root, owner)
    fresh = decay_rate * momentum + (1.0 - decay_rate) * mine.astype(jnp.float32)
    factor = 1.0 - jnp.power(jnp.float32(decay_rate), step.astype(jnp.float32))
    update = (fresh / factor).astype(jnp.bfloat16)
    return (fresh, update)


def solution(mesh):
    return jax.shard_map(
        body,
        mesh=mesh,
        in_specs=(
            P("rep", None, "dp"),
            P(),
            P("dp", None, "rep", None),
            P("dp", None, None, "rep"),
            P(None, ("rep", "dp")),
            P(),
        ),
        out_specs=(P(None, ("rep", "dp")), P(None, ("rep", "dp"))),
        check_vma=False,
    )
```

```python
import functools

import jax
import jax.numpy as jnp
from jax import lax
from jax.experimental import pallas as pl
from jax.experimental.pallas import tpu as pltpu
from jax.sharding import PartitionSpec as P

BLOCK = 1024
MOST = 3
NX, NY, NZ, NR = 4, 4, 16, 8
NB = 64
MESH = pl.DeviceIdType.MESH
Z_ORDER = (8, 7, 9, 6, 10, 5, 11, 4, 12, 3, 13, 2, 14, 1, 15)
GATE = Z_ORDER[:7]


decay_rate = 0.5


def block_tables(cap, owner, tab):
    def spread(b, both):
        row, col = both
        return jnp.where(lane == b, owner[b], row), jnp.where(sub == b, owner[b], col)

    sub = lax.broadcasted_iota(jnp.int32, (NB, 128), 0)
    lane = lax.broadcasted_iota(jnp.int32, (NB, 128), 1)
    none = jnp.full((NB, 128), -1, jnp.int32)
    row, col = lax.fori_loop(0, NB, spread, (none, none))
    one = jnp.ones((NB, 128), jnp.int32)
    held = row >= 0
    same = held & (row == col)
    slot = jnp.sum(jnp.where(same & (lane < sub), one, 0), axis=1, keepdims=True)
    slot_row = jnp.sum(jnp.where(same & (sub < lane), one, 0), axis=0, keepdims=True)
    peers = held & ((row & 15) == (col & 15)) & (slot_row == slot) & (row < col)
    rank = jnp.sum(jnp.where(peers, one, 0), axis=1, keepdims=True)
    line = col[:, :1]
    x, z = line // NZ, line & 15
    j = jnp.where(slot == 0, x, jnp.minimum(rank, cap - 1))
    place = z * 16 + jnp.minimum(slot, MOST - 1) * 4 + j
    block = lax.broadcasted_iota(jnp.int32, (NB, 1), 0)
    index = lax.broadcasted_iota(jnp.int32, (NB, 256), 1)
    tab[...] = jnp.zeros_like(tab)
    rows = (
        (place, block, NB - 1),
        (z * 16 + slot * 4 + x, j, cap - 1),
        (place, x, NX - 1),
        (block, place, NZ * 16 - 1),
    )
    for i, (key, value, top) in enumerate(rows):
        tab[i : i + 1, :] = jnp.minimum(jnp.sum(jnp.where(index == key, value, 0), axis=0, keepdims=True), top)


def step_kernel(
    cap, grads, left, right, owner_in, out,
    owner, vtab, tab, gbuf, s_a, r_a, s_b, r_b, tsc, gt, s_z, r_z0, r_z1, r_z2, s_x, gfull, lrow, rfull,
    s_e, r_e0, r_e1, r_e2, s_q, r_q,
    load_sem, a1s, a1r, a2s, a2r, z1s, z1r, x1s, x1r, ns, nr, hs, hr, cs, cr, e1s, e1r, e2s, e2r,
):
    caps = (NX, cap, cap)
    starts = (0, NX, NX + cap)
    rep, dp = lax.axis_index("rep"), lax.axis_index("dp")
    y, c = rep // 2, rep % 2
    x, z = dp // NZ, dp % NZ

    def at(dx=0, dy=0, dz=0, dc=0):
        return (((y + dy) % NY) * 2 + (c + dc) % 2, ((x + dx) % NX) * NZ + (z + dz) % NZ)

    def remote(src, dst, send, recv, device):
        return pltpu.make_async_remote_copy(
            src_ref=src, dst_ref=dst, send_sem=send, recv_sem=recv, device_id=device, device_id_type=MESH
        )

    load_o = pltpu.make_async_copy(owner_in, owner, load_sem.at[3])
    load_o.start()
    load_g = pltpu.make_async_copy(grads.at[0], gbuf, load_sem.at[0])
    load_g.start()
    load_l = pltpu.make_async_copy(left.at[0], lrow, load_sem.at[1])
    load_l.start()
    load_r = pltpu.make_async_copy(right.at[0], rfull.at[:, rep], load_sem.at[2])
    load_r.start()

    barrier = pltpu.get_barrier_semaphore()
    peers = [at(dz=k) for k in Z_ORDER] + [at(dx=k) for k in (2, 1, 3)]
    peers += [at(dy=k) for k in (1, 2, 3)] + [at(dc=1)]
    for peer in peers:
        pl.semaphore_signal(barrier, inc=1, device_id=peer, device_id_type=MESH)

    links = {}
    loads = {"left": load_l, "right": load_r, "owner": load_o}

    def go(name, out, back):
        out.start()
        links[name] = [out, back, True, True]

    def arrive(*name):
        links[name][1].wait_recv()
        links[name][2] = False

    def left(*name):
        links[name][0].wait_send()
        links[name][3] = False

    def loaded(name):
        loads.pop(name).wait()

    def finish():
        for copy in loads.values():
            copy.wait()
        for out, back, due, sent in links.values():
            if due:
                back.wait_recv()
            if sent:
                out.wait_send()

    def chunk(j, k, core):
        column = 8 * j + 2 * ((y + k) % NY) + core
        return gbuf[:, pl.ds(pl.multiple_of(128 * column, 128), 128)]

    def part(m, r, half=None):
        if m < MOST:
            return rfull.at[m, r] if half is None else rfull.at[m, r, pl.ds(half * 512, 512)]
        return gfull.at[m - MOST, r] if half is None else gfull.at[m - MOST, r, pl.ds(2 * half, 2)]

    def rep_of(dy, core):
        return ((y + dy) % NY) * 2 + core

    def near(m):
        for up in (1, 0):

            def copy(r, up=up):
                return remote(part(m, r), part(m, r), ns.at[m, up], nr.at[m, up], at(dy=1 if up else 3))

            go(("near", m, up), copy(rep), copy(rep_of(3 if up else 1, c)))
        cross(m, 0)

    def far(m, up):
        def copy(r):
            return remote(part(m, r, up), part(m, r, up), hs.at[m, up], hr.at[m, up], at(dy=1 if up else 3))

        go(("far", m, up), copy(rep_of(3 if up else 1, c)), copy(rep_of(2, c)))

    def cross(m, k):
        def copy(core):
            r = rep_of(k, core)
            return remote(part(m, r), part(m, r), cs.at[m, k], cr.at[m, k], at(dc=1))

        go(("cross", m, k), copy(c), copy(1 - c))

    def forward(m):
        for up in (1, 0):
            arrive("near", m, up)
            far(m, up)
        cross(m, 3)
        cross(m, 1)

    def last(m):
        arrive("far", m, 1)
        arrive("far", m, 0)
        cross(m, 2)

    def whole(m):
        for k in range(NY):
            arrive("cross", m, k)

    with jax.named_scope("pair_pack"):
        load_g.wait()
        for k in (2, 1, 3, 0):

            @pl.loop(0, 16)
            def _(j, k=k):
                s_a[k, j] = chunk(j, k, 1 - c)

    with jax.named_scope("barrier"):
        pl.semaphore_wait(barrier, len(peers))

    with jax.named_scope("pair_sum"):
        for k in (2, 1, 3, 0):
            copy = remote(s_a.at[k], r_a.at[k], a1s.at[k], a1r.at[k], at(dc=1))
            go(("a1", k), copy, copy)
        loaded("right")
        near(0)
        for k in (2, 1, 3):
            arrive("a1", k)

            @pl.loop(0, 16)
            def _(j, k=k):
                total = chunk(j, k, c).astype(jnp.float32) + r_a[k, j].astype(jnp.float32)
                s_b[k, j] = total.astype(jnp.bfloat16)

            copy = remote(s_b.at[k], r_b.at[k], a2s.at[k], a2r.at[k], at(dy=k))
            go(("a2", k), copy, copy)

    with jax.named_scope("tables"):
        loaded("owner")
        block_tables(cap, owner, vtab)
        to_smem = pltpu.make_async_copy(vtab, tab, load_sem.at[4])
        to_smem.start()
        loads["tables"] = to_smem

    with jax.named_scope("y_sum"):
        arrive("a1", 0)
        for k in (1, 2, 3):
            arrive("a2", k)

        @pl.loop(0, 16)
        def _(j):
            total = chunk(j, 0, c).astype(jnp.float32) + r_a[0, j].astype(jnp.float32)
            for k in (1, 2, 3):
                total += r_b[k, j].astype(jnp.float32)
            tsc[pl.ds(j, NB, stride=16), :] = total

        gt[...] = tsc[...].astype(jnp.bfloat16).reshape(NB, 16, 128)
        loaded("tables")

    r_z, r_e = (r_z0, r_z1, r_z2), (r_e0, r_e1, r_e2)

    def to_plane(s):
        for k in Z_ORDER + (0,):

            @pl.loop(0, caps[s])
            def _(e, k=k):
                tile = gt[tab[0, ((z + k) % NZ) * 16 + 4 * s + e]]
                if k:
                    s_z[k, starts[s] + e] = tile
                else:
                    r_z[s][0, e] = tile

            if k:
                copy = remote(s_z.at[k, pl.ds(starts[s], caps[s])], r_z[s].at[k], z1s.at[s, k], z1r.at[s, k], at(dz=k))
                go(("z1", s, k), copy, copy)

    def to_owner(s):
        for k in range(1, NZ):
            arrive("z1", s, k)
        for k in (2, 1, 3, 0):
            to = (x + k) % NX

            @pl.loop(0, NZ)
            def _(i, k=k, to=to):
                tile = r_z[s][i, tab[1, z * 16 + 4 * s + to] if s else to]
                rows = pl.ds(pl.multiple_of(16 * ((z + NZ - i) % NZ), 16), 16)
                if k:
                    s_x[k, s, rows] = tile
                else:
                    gfull[s, rep, x, rows] = tile

            if k:

                def x1(to, k=k):
                    return remote(s_x.at[k, s], gfull.at[s, rep, to], x1s.at[s, k], x1r.at[s, k], at(dx=k))

                go(("x1", s, k), x1(x), x1((x + NX - k) % NX))

    def at_owner(s):
        for k in range(1, NX):
            arrive("x1", s, k)
        near(MOST + s)

    def products(s):
        whole(s)
        whole(MOST + s)
        w = []
        for p in range(4):
            cols = jnp.concatenate([gfull[s, 2 * p + i].reshape(BLOCK, 128) for i in range(2)], axis=1)
            w.append(jnp.dot(lrow[s], cols, preferred_element_type=jnp.float32).astype(jnp.bfloat16))
        w = jnp.concatenate(w, axis=1)
        for p in range(4):
            cols = jnp.concatenate([rfull[s, 2 * p], rfull[s, 2 * p + 1]], axis=1)
            d = jnp.dot(w, cols, preferred_element_type=jnp.float32)
            tsc[pl.ds(2 * p, 128, stride=8), :] = d[:, :128]
            tsc[pl.ds(2 * p + 1, 128, stride=8), :] = d[:, 128:]
        s_e[s] = tsc[...].astype(jnp.bfloat16).reshape(NX, NZ, 16, 128)
        for k in (2, 1, 3):

            def e1(to, come, k=k):
                return remote(s_e.at[s, to], r_e[s].at[come], e1s.at[s, k], e1r.at[s, k], at(dx=k))

            go(("e1", s, k), e1((x + k) % NX, x), e1(x, (x + NX - k) % NX))
        r_e[s][x] = s_e[s, x]

    def from_owner(s):
        for k in range(1, NX):
            arrive("e1", s, k)
        for k in Z_ORDER + (0,):

            @pl.loop(0, caps[s])
            def _(e, k=k):
                tile = r_e[s][tab[2, z * 16 + 4 * s + e] if s else e, (z + k) % NZ]
                if k:
                    s_q[k, starts[s] + e] = tile
                else:
                    r_q[0, starts[s] + e] = tile

            if k:
                mine = pl.ds(starts[s], caps[s])
                copy = remote(s_q.at[k, mine], r_q.at[k, mine], e2s.at[s, k], e2r.at[s, k], at(dz=k))
                go(("e2", s, k), copy, copy)

    def gate(s):
        for k in GATE:
            left("z1", s, k)

    with jax.named_scope("out"):
        to_plane(0)
        near(1)
        near(2)
        forward(0)
    with jax.named_scope("out_1"):
        gate(0)
        to_plane(1)
        forward(1)
        forward(2)
        to_owner(0)
    with jax.named_scope("out_2"):
        gate(1)
        to_plane(2)
        at_owner(0)
        for s in range(MOST):
            last(s)
    with jax.named_scope("gather"):
        to_owner(1)
        forward(3)
        at_owner(1)
        to_owner(2)
        last(3)
        forward(4)
        at_owner(2)
    with jax.named_scope("product_0"):
        loaded("left")
        products(0)
    with jax.named_scope("gather_2"):
        last(4)
        forward(5)
        from_owner(0)
    with jax.named_scope("product_1"):
        products(1)
        last(5)
        from_owner(1)
    with jax.named_scope("product_2"):
        products(2)
        from_owner(2)
    with jax.named_scope("at_shards"):
        for s in range(MOST):
            for k in range(1, NZ):
                arrive("e2", s, k)
    with jax.named_scope("pick"):

        @pl.loop(0, NB)
        def _(b):
            v = tab[3, b]
            place = v % 16
            tile = r_q[(z + NZ - v // 16) % NZ, place - (place // 8) * (NX - cap)]
            tsc[pl.ds(pl.multiple_of(16 * b, 16), 16), :] = tile.astype(jnp.float32)

        for j in range(16):
            out[:, 128 * j : 128 * (j + 1)] = tsc[pl.ds(j, NB, stride=16), :].astype(jnp.bfloat16)

    with jax.named_scope("sends_done"):
        finish()


def directions(cap, cid, grads, left, right, owner):
    bf16, f32, dma = jnp.bfloat16, jnp.float32, pltpu.SemaphoreType.DMA
    hbm = pl.BlockSpec(memory_space=pl.ANY)
    return pl.pallas_call(
        functools.partial(step_kernel, cap),
        out_shape=jax.ShapeDtypeStruct((NB, 2048), bf16),
        in_specs=[hbm] * 4,
        out_specs=pl.BlockSpec(memory_space=pltpu.VMEM),
        scratch_shapes=[
            pltpu.SMEM((NB,), jnp.int32),
            pltpu.VMEM((8, 256), jnp.int32),
            pltpu.SMEM((8, 256), jnp.int32),
            pltpu.VMEM((NB, 16384), bf16),
            pltpu.VMEM((NY, 16, NB, 128), bf16),
            pltpu.VMEM((NY, 16, NB, 128), bf16),
            pltpu.VMEM((NY, 16, NB, 128), bf16),
            pltpu.VMEM((NY, 16, NB, 128), bf16),
            pltpu.VMEM((BLOCK, 128), f32),
            pltpu.VMEM((NB, 16, 128), bf16),
            pltpu.VMEM((NZ, NX + 2 * cap, 16, 128), bf16),
            pltpu.VMEM((NZ, NX, 16, 128), bf16),
            pltpu.VMEM((NZ, cap, 16, 128), bf16),
            pltpu.VMEM((NZ, cap, 16, 128), bf16),
            pltpu.VMEM((NX, MOST, 256, 128), bf16),
            pltpu.VMEM((MOST, NR, NX, 256, 128), bf16),
            pltpu.VMEM((MOST, 128, BLOCK), bf16),
            pltpu.VMEM((MOST, NR, BLOCK, 128), bf16),
            pltpu.VMEM((MOST, NX, NZ, 16, 128), bf16),
            pltpu.VMEM((NX, NZ, 16, 128), bf16),
            pltpu.VMEM((NX, NZ, 16, 128), bf16),
            pltpu.VMEM((NX, NZ, 16, 128), bf16),
            pltpu.VMEM((NZ, NX + 2 * cap, 16, 128), bf16),
            pltpu.VMEM((NZ, NX + 2 * cap, 16, 128), bf16),
            dma((5,)),
            dma((NY,)), dma((NY,)),
            dma((NY,)), dma((NY,)),
            dma((MOST, NZ)), dma((MOST, NZ)),
            dma((MOST, NX)), dma((MOST, NX)),
            dma((2 * MOST, 2)), dma((2 * MOST, 2)),
            dma((2 * MOST, 2)), dma((2 * MOST, 2)),
            dma((2 * MOST, NY)), dma((2 * MOST, NY)),
            dma((MOST, NX)), dma((MOST, NX)),
            dma((MOST, NZ)), dma((MOST, NZ)),
        ],
        compiler_params=pltpu.CompilerParams(
            collective_id=cid, has_side_effects=True, vmem_limit_bytes=48 * 2**20
        ),
        name=f"directions_{cap}",
    )(grads, left, right, owner)


CAPS = (3, NX)


def body(grads, owner, left_root, right_root, momentum, step):
    lines = jnp.arange(NX * NZ, dtype=jnp.int32).reshape(NX, NZ, 1)
    held = jnp.sum((owner == lines).astype(jnp.int32), axis=2)
    most = jnp.max(jnp.sum((held > 1).astype(jnp.int32), axis=0))
    which = sum((most > cap).astype(jnp.int32) for cap in CAPS[:-1])
    branches = [functools.partial(directions, cap, i) for i, cap in enumerate(CAPS)]
    mine = lax.switch(which, branches, grads, left_root, right_root, owner)
    fresh = decay_rate * momentum + (1.0 - decay_rate) * mine.astype(jnp.float32)
    factor = 1.0 - jnp.power(jnp.float32(decay_rate), step.astype(jnp.float32))
    update = (fresh / factor).astype(jnp.bfloat16)
    return (fresh, update)


def solution(mesh):
    return jax.shard_map(
        body,
        mesh=mesh,
        in_specs=(
            P("rep", None, "dp"),
            P(),
            P("dp", None, "rep", None),
            P("dp", None, None, "rep"),
            P(None, ("rep", "dp")),
            P(),
        ),
        out_specs=(P(None, ("rep", "dp")), P(None, ("rep", "dp"))),
        check_vma=False,
    )
```
